256 devices in a mesh: hst: 16 (over x, y), chip: 16 (over z, core).
Axes of the slice: x: 4, y: 4, z: 8, core: 2. Of those that a mesh axis runs over, the one named last changes fastest.
Arguments:
- top_input: bfloat16 [32768, 2048], P(('hst', 'chip')), may hold values from -24 to 24
- grad_hidden: bfloat16 [32768, 2048], P(('hst', 'chip')), may hold values from -0.59765625 to 0.59765625
- w_in: bfloat16 [2048, 2048], replicated, may hold values from -0.125 to 0.125
- b_in: float32 [2048], replicated, may hold values from -3 to 3
- slice_map: int32 [16], replicated, may hold values from 0 to 15, as said below
- lookup_ids: int32 [16, 4, 32768], P('hst'), may hold values from 0 to 4095
- bag_len: int32 [16, 32768], P('hst'), may hold values from 1 to 4
Outputs:
- w_in_grad: float32 [2048, 2048], P(('hst', 'chip'))
- table_grad: float32 [16, 4096, 128], P('hst', 'chip')
The draws below stay inside these ranges and needn't reach their ends.
Inputs may be any that keep to these rules, and one draw needn't show every extreme that they name: slice_map is a permutation; slice s holds half slice_map[s] % 2 of table slice_map[s] // 2, and two slices of one table have the same lookup_ids and bag_len.
All inputs are finite; a program needn't handle non-finite values.
Results may differ from the reference program's by a relative error of at most 0.0041.
Values may be sent and summed in bfloat16 or wider, within the bound.
No kernel may reach another device: no remote copies, remote signals or barrier semaphores. Data moves between devices by JAX's collectives and lax.ppermute only.
A program may use at most 128 MiB of HBM per device.

```python
import jax
import jax.numpy as jnp
from jax import lax

SLW = 128
H = 2048
BAG = 4
SLICES = 16
TABLES = 8
Z = 2048
B = 32768
ROWS = 4096


def slice_table(key):
    return jax.random.permutation(jax.random.fold_in(key, 11), SLICES).astype(jnp.int32)


def table_lookups(key):
    first_key, second_key, shift_key, len_key = jax.random.split(jax.random.fold_in(key, 12), 4)
    first = jax.random.randint(first_key, (TABLES, BAG, B), 0, ROWS)
    second = jax.random.randint(second_key, (TABLES, BAG, B), 0, ROWS)
    offset = jax.random.randint(shift_key, (TABLES, 1, 1), 0, ROWS)
    row_ids = (jnp.minimum(first, second) + offset) % ROWS
    bag_lens = jax.random.randint(len_key, (TABLES, B), 1, BAG + 1)
    bag_lens = bag_lens.at[:, 0].set(BAG)
    return (row_ids.astype(jnp.int32), bag_lens.astype(jnp.int32))


def draw_slice_map(key, part):
    order = slice_table(key)
    return order


def draw_lookup_ids(key, part):
    order = slice_table(key)
    row_ids, bag_lens = table_lookups(key)
    return row_ids[order // 2]


def draw_bag_len(key, part):
    order = slice_table(key)
    row_ids, bag_lens = table_lookups(key)
    return bag_lens[order // 2]


def with_spikes(array, stream_key, source, target, parts, factor):
    owner, partner = [(jnp.arange(array.shape[dim]) // (array.shape[dim] // parts)).reshape([-1 if axis == dim else 1 for axis in range(array.ndim)]) for dim in (source, target)]
    chosen = jax.random.permutation(stream_key, parts)[partner]
    strong = (owner == chosen) | (owner == (partner + parts // 2) % parts)
    return jnp.where(strong, factor * array, array)


def block_levels(stream_key, extent, pieces, smallest, top_value):
    def one(position, shards_of):
        draws = jax.random.uniform(jax.random.fold_in(jax.random.fold_in(stream_key, 6), position), (shards_of,), jnp.float32, smallest / len(pieces), top_value / len(pieces))
        return jnp.repeat(jnp.exp(draws), extent[position] // shards_of).reshape((-1,) + (1,) * (len(extent) - position - 1))

    loudness = one(*pieces[0])
    for cut in pieces[1:]:
        loudness = loudness * one(*cut)
    return loudness


def scatter_about(rng, dims, deviation, reach, shards=(), held_as=jnp.bfloat16):
    values = jax.random.normal(rng, dims, jnp.float32) * deviation
    if len(shards) > 0:
        values = block_levels(rng, dims, shards, -0.22, 0.18) * values
    return jnp.clip(values, min=-reach, max=reach).astype(held_as)


def heavy_noise(own_key, shape, scale, reach, pieces, heavy, kind=jnp.bfloat16):
    values = scale * jax.random.normal(own_key, shape, jnp.float32)
    if pieces:
        values = values * block_levels(own_key, shape, pieces, -0.22, 0.18)
    return jnp.clip(with_spikes(values, jax.random.fold_in(own_key, 3), *heavy), -reach, reach).astype(kind)


def setup_inputs(seed: int = 0) -> dict:
    seeds = jax.random.split(jax.random.key(seed), 8)
    top_input = heavy_noise(seeds[0], (B, Z), 1.0, 24.0, ((0, 256),), (0, 1, 256, 6.0))
    grad_hidden = scatter_about(seeds[1], (B, H), 0.1, 0.59765625, ((0, 256),))
    w_in = scatter_about(seeds[2], (Z, H), Z ** -0.5, 0.125)
    b_in = scatter_about(seeds[3], (H,), 0.5, 3.0, (), jnp.float32)
    slice_map = draw_slice_map(jax.random.fold_in(seeds[7], 71), 0)
    lookup_ids = draw_lookup_ids(jax.random.fold_in(seeds[7], 71), 0)
    bag_len = draw_bag_len(jax.random.fold_in(seeds[7], 71), 0)
    return {"top_input": top_input, "grad_hidden": grad_hidden, "w_in": w_in, "b_in": b_in, "slice_map": slice_map, "lookup_ids": lookup_ids, "bag_len": bag_len}


def reference(top_input, grad_hidden, w_in, b_in, slice_map, lookup_ids, bag_len):
    pre_act = jnp.dot(top_input, w_in, preferred_element_type=jnp.float32) + b_in
    gate_sig = jax.nn.sigmoid(pre_act)
    grad_pre = (grad_hidden.astype(jnp.float32) * gate_sig * (1.0 + pre_act * (1.0 - gate_sig))).astype(jnp.bfloat16)
    w_in_grad = jnp.dot(top_input.T, grad_pre, preferred_element_type=jnp.float32)
    pooled = jnp.dot(grad_pre, w_in.T, preferred_element_type=jnp.float32).astype(jnp.bfloat16)

    def slice_grads(item):
        block, row_ids, bag_lens = item
        columns = lax.dynamic_slice_in_dim(pooled, block * SLW, SLW, 1).astype(jnp.float32)
        live = (jnp.arange(BAG, dtype=jnp.int32)[:, None] < bag_lens[None, :]).astype(jnp.float32)
        total = jnp.zeros((ROWS, SLW), jnp.float32)
        for slot in range(BAG):
            total = total + jax.ops.segment_sum(columns * live[slot][:, None], row_ids[slot], num_segments=ROWS)
        return total

    table_grad = lax.map(slice_grads, (slice_map.astype(jnp.int32), lookup_ids, bag_len))
    return w_in_grad, table_grad
```

```python
import functools

import jax
import jax.numpy as jnp
from jax import lax
from jax.experimental import pallas as pl
from jax.experimental.pallas import tpu as pltpu
from jax.sharding import PartitionSpec as P

NX, NY, NZ, NC = 4, 4, 8, 2
AXES = ("hst", "chip")
ROWS_DEV = 256
LOCAL_ROWS = NZ * ROWS_DEV


def device_index(x, y, z, c):
    return ((x * NY + y) * NZ + z) * NC + c


def shift_perm(dx=0, dy=0, dc=0):
    pairs = []
    for x in range(NX):
        for y in range(NY):
            for z in range(NZ):
                for c in range(NC):
                    pairs.append(
                        (
                            device_index(x, y, z, c),
                            device_index((x + dx) % NX, (y + dy) % NY, z, (c + dc) % NC),
                        )
                    )
    return pairs


def send(value, **shift):
    return lax.ppermute(value, AXES, shift_perm(**shift))


def table_kernel(chunk, rb, ids_ref, x_ref, o_ref):
    samples = x_ref.shape[0]
    one = jnp.ones((), jnp.bfloat16)
    zero = jnp.zeros((), jnp.bfloat16)
    target = lax.broadcasted_iota(jnp.int32, (rb, chunk), 0).astype(jnp.int16)

    def do_block(k, carry):
        base = k * rb
        acc = jnp.zeros((rb, x_ref.shape[1]), jnp.float32)
        for s in range(samples // chunk):
            ids = (ids_ref[:, s * chunk : (s + 1) * chunk] - base).astype(jnp.int16)
            counts = None
            for j in range(ids_ref.shape[0]):
                hit = jnp.where(jnp.broadcast_to(ids[j : j + 1], (rb, chunk)) == target, one, zero)
                counts = hit if counts is None else counts + hit
            acc = acc + jnp.dot(
                counts, x_ref[s * chunk : (s + 1) * chunk, :], preferred_element_type=jnp.float32
            )
        o_ref[pl.ds(pl.multiple_of(base, rb), rb), :] = acc
        return carry

    lax.fori_loop(0, o_ref.shape[0] // rb, do_block, 0)


def table_partial(ids, x):
    return pl.pallas_call(
        functools.partial(table_kernel, 256, 512),
        out_shape=jax.ShapeDtypeStruct((LOCAL_ROWS, x.shape[1]), jnp.float32),
        in_specs=[pl.BlockSpec(memory_space=pltpu.VMEM)] * 2,
        out_specs=pl.BlockSpec(memory_space=pltpu.VMEM),
        compiler_params=pltpu.CompilerParams(vmem_limit_bytes=32 << 20),
        name="table_partial",
    )(ids, x)


def f32(v):
    return v.astype(jnp.float32)


def body(top_input, grad_hidden, w_in, b_in, slice_map, lookup_ids, bag_len):
    hst = lax.axis_index("hst")
    chip = lax.axis_index("chip")
    x, y = hst // NY, hst % NY
    z, core = chip // NC, chip % NC
    b_dev, width = top_input.shape
    hidden = grad_hidden.shape[1]
    slices = slice_map.shape[0]
    slw = width // slices
    half = hidden // NC
    quart = half // 2

    top_other = send(top_input, dc=1)
    pre_act = jnp.dot(top_input, w_in, preferred_element_type=jnp.float32) + b_in
    gate_sig = jax.nn.sigmoid(pre_act)
    grad_pre = (f32(grad_hidden) * gate_sig * (1.0 + pre_act * (1.0 - gate_sig))).astype(jnp.bfloat16)
    grad_mine = lax.dynamic_slice_in_dim(grad_pre, core * half, half, 1)
    grad_other = send(lax.dynamic_slice_in_dim(grad_pre, (1 - core) * half, half, 1), dc=1)
    pooled = lax.dot_general(
        grad_pre, w_in, (((1,), (1,)), ((), ())), preferred_element_type=jnp.float32
    ).astype(jnp.bfloat16)

    top_chip = jnp.concatenate([top_input, top_other], axis=0)
    grad_chip = jnp.concatenate([grad_mine, grad_other], axis=0)
    part = lax.dot_general(
        top_chip, grad_chip, (((0,), (0,)), ((), ())), preferred_element_type=jnp.float32
    ).astype(jnp.bfloat16)
    part = part.reshape(NX, NY, width // (NX * NY), half)
    part_a, part_b = part[..., :quart], part[..., quart:]

    def take(v, axis, index):
        return lax.dynamic_index_in_dim(v, index, axis, keepdims=False)

    got_a = [send(take(part_a, 0, (x + d) % NX), dx=d) for d in (1, 3, 2)]
    got_b = [send(take(part_b, 1, (y + d) % NY), dy=d) for d in (1, 3, 2)]

    selector = (slice_map[:, None] == lax.iota(jnp.int32, slices)[None, :]).astype(jnp.bfloat16)
    ordered = jnp.einsum(
        "bkc,sk->sbc",
        pooled.reshape(b_dev, slices, slw),
        selector,
        preferred_element_type=jnp.float32,
    ).astype(jnp.bfloat16)
    received = lax.all_to_all(ordered, "hst", split_axis=0, concat_axis=1, tiled=True)[0]
    rec_other = send(received, dc=1)

    slots = lookup_ids.shape[1]
    ids = lookup_ids[0].reshape(slots, NX * NY, NZ, NC, b_dev)
    lens = bag_len[0].reshape(NX * NY, NZ, NC, b_dev)
    ids = lax.dynamic_index_in_dim(ids, z, 2, keepdims=False)
    lens = lax.dynamic_index_in_dim(lens, z, 1, keepdims=False)
    live = lax.iota(jnp.int32, slots)[:, None, None, None] < lens[None]
    here = (ids // ROWS_DEV) % NC == core
    local = (ids // (NC * ROWS_DEV)) * ROWS_DEV + ids % ROWS_DEV
    local = jnp.where(live & here, local, -1)
    mine = lax.dynamic_index_in_dim(local, core, 2, keepdims=False).reshape(slots, -1)
    theirs = lax.dynamic_index_in_dim(local, 1 - core, 2, keepdims=False).reshape(slots, -1)
    local = jnp.concatenate([mine, theirs], axis=1)
    table = table_partial(local, jnp.concatenate([received, rec_other], axis=0))
    groups = [[zz * NC + c for zz in range(NZ)] for c in range(NC)]
    table = lax.psum_scatter(
        table, "chip", scatter_dimension=0, axis_index_groups=groups, tiled=True
    )

    sum_a = (f32(take(part_a, 0, x)) + f32(got_a[0]) + f32(got_a[1]) + f32(got_a[2])).astype(jnp.bfloat16)
    sum_b = (f32(take(part_b, 1, y)) + f32(got_b[0]) + f32(got_b[1]) + f32(got_b[2])).astype(jnp.bfloat16)
    got_a = [send(take(sum_a, 0, (y + d) % NY), dy=d) for d in (1, 3, 2)]
    got_b = [send(take(sum_b, 0, (x + d) % NX), dx=d) for d in (1, 3, 2)]
    fin_a = f32(take(sum_a, 0, y)) + f32(got_a[0]) + f32(got_a[1]) + f32(got_a[2])
    fin_b = f32(take(sum_b, 0, x)) + f32(got_b[0]) + f32(got_b[1]) + f32(got_b[2])
    fin = jnp.concatenate([fin_a, fin_b], axis=1).astype(jnp.bfloat16)
    rows_out = fin.shape[0] // (NZ * NC)
    swapped = lax.all_to_all(
        fin.reshape(NZ * NC, rows_out, half), "chip", split_axis=0, concat_axis=0, tiled=True
    )
    total = f32(swapped).reshape(NZ, NC, rows_out, half).sum(0)
    w_in_grad = total.transpose(1, 0, 2).reshape(rows_out, hidden)
    return (w_in_grad, table[None])


def solution(mesh):
    in_specs = (
        P(("hst", "chip"), None),
        P(("hst", "chip"), None),
        P(),
        P(),
        P(),
        P("hst", None, None),
        P("hst", None),
    )
    out_specs = (P(("hst", "chip"), None), P("hst", "chip", None))
    return jax.shard_map(body, mesh=mesh, in_specs=in_specs, out_specs=out_specs, check_vma=False)
```

```python
import functools

import jax
import jax.numpy as jnp
from jax import lax
from jax.experimental import pallas as pl
from jax.experimental.pallas import tpu as pltpu
from jax.sharding import PartitionSpec as P

NX, NY, NZ, NC = 4, 4, 8, 2
AXES = ("hst", "chip")
ROWS_DEV = 256
LOCAL_ROWS = NZ * ROWS_DEV
VMEM = pl.BlockSpec(memory_space=pltpu.VMEM)


def device_index(x, y, z, c):
    return ((x * NY + y) * NZ + z) * NC + c


def permutation(target):
    pairs = []
    for x in range(NX):
        for y in range(NY):
            for z in range(NZ):
                for c in range(NC):
                    pairs.append((device_index(x, y, z, c), device_index(*target(x, y, z, c))))
    return pairs


def core_swap(value):
    return lax.ppermute(value, AXES, permutation(lambda x, y, z, c: (x, y, z, 1 - c)))


def pair_swap(value):
    return lax.ppermute(value, AXES, permutation(lambda x, y, z, c: (x, y, z ^ 1, c)))


def z_shift(value, d):
    return lax.ppermute(value, AXES, permutation(lambda x, y, z, c: (x, y, (z + d) % NZ, c)))


def f32(v):
    return v.astype(jnp.float32)


def params(mib):
    return pltpu.CompilerParams(vmem_limit_bytes=mib << 20)


def weight_kernel(x0, x1, x2, x3, g0, g1, g2, g3, o_ref):
    grads = jnp.concatenate([g[...] for g in (g0, g1, g2, g3)], axis=0)
    step = 512
    for first in range(0, x0.shape[1], step):
        left = jnp.concatenate([v[:, first : first + step] for v in (x0, x1, x2, x3)], axis=0)
        o_ref[first : first + step, :] = lax.dot_general(
            left, grads, (((0,), (0,)), ((), ())), preferred_element_type=jnp.float32
        ).astype(jnp.bfloat16)


def weight_part(tops, grads):
    return pl.pallas_call(
        weight_kernel,
        out_shape=jax.ShapeDtypeStruct((tops[0].shape[1], grads[0].shape[1]), jnp.bfloat16),
        in_specs=[VMEM] * 8,
        out_specs=VMEM,
        compiler_params=params(32),
        name="weight_part",
    )(*tops, *grads)


def table_kernel(chunk, rb, ids_ref, x_ref, y_ref, o_ref):
    samples = x_ref.shape[0]
    one = jnp.ones((), jnp.bfloat16)
    zero = jnp.zeros((), jnp.bfloat16)
    target = lax.broadcasted_iota(jnp.int32, (rb, chunk), 0).astype(jnp.int16)

    def do_block(k, carry):
        base = k * rb
        acc = jnp.zeros((rb, x_ref.shape[1]), jnp.float32)
        for s in range(2 * samples // chunk):
            ids = (ids_ref[:, s * chunk : (s + 1) * chunk] - base).astype(jnp.int16)
            counts = None
            for j in range(ids_ref.shape[0]):
                hit = jnp.where(jnp.broadcast_to(ids[j : j + 1], (rb, chunk)) == target, one, zero)
                counts = hit if counts is None else counts + hit
            first = s * chunk
            rows = x_ref[first : first + chunk, :] if first < samples else y_ref[first - samples : first - samples + chunk, :]
            acc = acc + jnp.dot(counts, rows, preferred_element_type=jnp.float32)
        o_ref[pl.ds(pl.multiple_of(base, rb), rb), :] = acc.astype(jnp.bfloat16)
        return carry

    lax.fori_loop(0, o_ref.shape[0] // rb, do_block, 0)


def table_partial(ids, x, y):
    return pl.pallas_call(
        functools.partial(table_kernel, 256, 512),
        out_shape=jax.ShapeDtypeStruct((LOCAL_ROWS, x.shape[1]), jnp.bfloat16),
        in_specs=[VMEM] * 3,
        out_specs=VMEM,
        compiler_params=params(32),
        name="table_partial",
    )(ids, x, y)


def body(top_input, grad_hidden, w_in, b_in, slice_map, lookup_ids, bag_len):
    chip = lax.axis_index("chip")
    z, core = lax.div(chip, NC), lax.rem(chip, NC)
    bit = lax.rem(z, 2)
    b_dev, width = top_input.shape
    hidden = grad_hidden.shape[1]
    slices = slice_map.shape[0]
    slw = width // slices
    half = hidden // 2
    quart = half // NC

    top_core = core_swap(top_input)
    top_pair = pair_swap(top_input)
    top_both = core_swap(top_pair)

    pre_act = jnp.dot(top_input, w_in, preferred_element_type=jnp.float32) + b_in
    gate_sig = jax.nn.sigmoid(pre_act)
    grad_pre = (f32(grad_hidden) * gate_sig * (1.0 + pre_act * (1.0 - gate_sig))).astype(jnp.bfloat16)

    keep = lax.dynamic_slice_in_dim(grad_pre, bit * half, half, 1)
    pair = pair_swap(lax.dynamic_slice_in_dim(grad_pre, (1 - bit) * half, half, 1))

    def mine(v):
        return lax.dynamic_slice_in_dim(v, core * quart, quart, 1)

    def other(v):
        return lax.dynamic_slice_in_dim(v, (1 - core) * quart, quart, 1)

    grads = (mine(keep), core_swap(other(keep)), mine(pair), core_swap(other(pair)))
    part = weight_part((top_input, top_core, top_pair, top_both), grads)

    pooled = lax.dot_general(
        grad_pre, w_in, (((1,), (1,)), ((), ())), preferred_element_type=jnp.float32
    ).astype(jnp.bfloat16)
    selector = (slice_map[:, None] == lax.iota(jnp.int32, slices)[None, :]).astype(jnp.bfloat16)
    ordered = jnp.einsum(
        "bkc,sk->sbc",
        pooled.reshape(b_dev, slices, slw),
        selector,
        preferred_element_type=jnp.float32,
    ).astype(jnp.bfloat16)
    received = lax.all_to_all(ordered, "hst", split_axis=0, concat_axis=1, tiled=True)[0]
    rec_other = core_swap(received)

    blocks = lax.all_to_all(
        part.reshape(NX * NY, width // (NX * NY), quart), "hst", split_axis=0, concat_axis=0, tiled=True
    )

    slots = lookup_ids.shape[1]
    ids = lookup_ids[0].reshape(slots, NX * NY, NZ, NC, b_dev)
    lens = bag_len[0].reshape(NX * NY, NZ, NC, b_dev)
    ids = lax.dynamic_index_in_dim(ids, z, 2, keepdims=False)
    lens = lax.dynamic_index_in_dim(lens, z, 1, keepdims=False)
    live = lax.iota(jnp.int32, slots)[:, None, None, None] < lens[None]
    here = (ids // ROWS_DEV) % NC == core
    local = (ids // (NC * ROWS_DEV)) * ROWS_DEV + ids % ROWS_DEV
    local = jnp.where(live & here, local, -1)
    near = lax.dynamic_index_in_dim(local, core, 2, keepdims=False).reshape(slots, -1)
    far = lax.dynamic_index_in_dim(local, 1 - core, 2, keepdims=False).reshape(slots, -1)
    local = jnp.concatenate([near, far], axis=1)
    table = table_partial(local, received, rec_other)
    table = table.reshape(NZ, ROWS_DEV, -1)

    def rows_of(d):
        return lax.dynamic_index_in_dim(table, lax.rem(z + d, NZ), 0, keepdims=False)

    table_grad = f32(rows_of(0))
    for d in (4, 3, 5, 2, 6, 1, 7):
        table_grad = table_grad + f32(z_shift(rows_of(d), d))

    summed = f32(blocks).sum(0).astype(jnp.bfloat16)
    rows_out = summed.shape[0] // (NZ * NC)
    swapped = lax.all_to_all(
        summed.reshape(NZ * NC, rows_out, quart), "chip", split_axis=0, concat_axis=0, tiled=True
    )
    total = f32(swapped).reshape(NZ // 2, 2 * NC, rows_out, quart).sum(0)
    w_in_grad = total.transpose(1, 0, 2).reshape(rows_out, hidden)
    return (w_in_grad, table_grad[None])


def solution(mesh):
    in_specs = (
        P(("hst", "chip"), None),
        P(("hst", "chip"), None),
        P(),
        P(),
        P(),
        P("hst", None, None),
        P("hst", None),
    )
    out_specs = (P(("hst", "chip"), None), P("hst", "chip", None))
    return jax.shard_map(body, mesh=mesh, in_specs=in_specs, out_specs=out_specs, check_vma=False)
```

```python
import functools

import jax
import jax.numpy as jnp
from jax import lax
from jax.experimental import pallas as pl
from jax.experimental.pallas import tpu as pltpu
from jax.sharding import PartitionSpec as P

NX, NY, NZ, NC = 4, 4, 8, 2
AXES = ("hst", "chip")
ROWS_DEV = 256
LOCAL_ROWS = NZ * ROWS_DEV
VMEM = pl.BlockSpec(memory_space=pltpu.VMEM)
HBM = pl.BlockSpec(memory_space=pltpu.MemorySpace.HBM)


def device_index(x, y, z, c):
    return ((x * NY + y) * NZ + z) * NC + c


def permutation(target):
    pairs = []
    for x in range(NX):
        for y in range(NY):
            for z in range(NZ):
                for c in range(NC):
                    pairs.append((device_index(x, y, z, c), device_index(*target(x, y, z, c))))
    return pairs


def core_swap(value):
    return lax.ppermute(value, AXES, permutation(lambda x, y, z, c: (x, y, z, 1 - c)))


def pair_swap(value):
    return lax.ppermute(value, AXES, permutation(lambda x, y, z, c: (x, y, z ^ 1, c)))


def z_shift(value, d):
    return lax.ppermute(value, AXES, permutation(lambda x, y, z, c: (x, y, (z + d) % NZ, c)))


def f32(v):
    return v.astype(jnp.float32)


def in_hbm(v):
    return pltpu.with_memory_space_constraint(v, pltpu.MemorySpace.HBM)


def params(mib):
    return pltpu.CompilerParams(vmem_limit_bytes=mib << 20)


def front_kernel(map_hbm, top_hbm, gh_hbm, w_hbm, b_hbm, gp_ref, out_ref, map_ref, top_ref, gh_ref, w_ref, b_ref, acc_ref, sems):
    hidden = gh_ref.shape[1]
    blocks = sems.shape[0] - 4
    block = hidden // blocks
    small = [
        pltpu.make_async_copy(src, dst, sems.at[k])
        for k, (src, dst) in enumerate(
            ((top_hbm, top_ref), (b_hbm, b_ref), (gh_hbm, gh_ref), (map_hbm, map_ref))
        )
    ]
    large = [
        pltpu.make_async_copy(
            w_hbm.at[:, pl.ds(j * block, block)],
            w_ref.at[:, pl.ds(j * block, block)],
            sems.at[4 + j],
        )
        for j in range(blocks)
    ]
    for copy in small[:1] + large[:1] + small[1:] + large[1:]:
        copy.start()
    for j in range(blocks):
        cols = slice(j * block, (j + 1) * block)
        if j == 0:
            small[0].wait()
        large[j].wait()
        w = w_ref[:, cols]
        pre = jnp.dot(top_ref[...], w, preferred_element_type=jnp.float32)
        if j == 0:
            for copy in small[1:]:
                copy.wait()
        pre = pre + b_ref[:, cols]
        sig = 1.0 / (1.0 + jnp.exp(-pre))
        grad = (f32(gh_ref[:, cols]) * sig * (1.0 + pre * (1.0 - sig))).astype(jnp.bfloat16)
        gp_ref[:, cols] = grad
        part = lax.dot_general(grad, w, (((1,), (1,)), ((), ())), preferred_element_type=jnp.float32)
        if j == 0:
            acc_ref[...] = part
        else:
            acc_ref[...] += part
    slw = out_ref.shape[2]
    for s in range(out_ref.shape[0]):
        first = pl.multiple_of(map_ref[s] * slw, slw)
        out_ref[s] = acc_ref[:, pl.ds(first, slw)].astype(jnp.bfloat16)


def front(slice_map, top_input, grad_hidden, w_in, b_in, blocks=4):
    b_dev, width = top_input.shape
    hidden = grad_hidden.shape[1]
    slices = slice_map.shape[0]
    slw = width // slices
    return pl.pallas_call(
        front_kernel,
        in_specs=[HBM] * 5,
        out_specs=[VMEM] * 2,
        out_shape=[
            jax.ShapeDtypeStruct((b_dev, hidden), jnp.bfloat16),
            jax.ShapeDtypeStruct((slices, b_dev, slw), jnp.bfloat16),
        ],
        scratch_shapes=[
            pltpu.SMEM((slices,), jnp.int32),
            pltpu.VMEM((b_dev, width), jnp.bfloat16),
            pltpu.VMEM((b_dev, hidden), jnp.bfloat16),
            pltpu.VMEM((width, hidden), jnp.bfloat16),
            pltpu.VMEM((1, hidden), jnp.float32),
            pltpu.VMEM((b_dev, width), jnp.float32),
            pltpu.SemaphoreType.DMA((4 + blocks,)),
        ],
        compiler_params=params(40),
        name="front",
    )(*[in_hbm(v) for v in (slice_map, top_input, grad_hidden, w_in, b_in[None])])


def weight_kernel(x0, x1, x2, x3, g0, g1, g2, g3, o_ref):
    grads = jnp.concatenate([g[...] for g in (g0, g1, g2, g3)], axis=0)
    step = 512
    for first in range(0, x0.shape[1], step):
        left = jnp.concatenate([v[:, first : first + step] for v in (x0, x1, x2, x3)], axis=0)
        o_ref[first : first + step, :] = lax.dot_general(
            left, grads, (((0,), (0,)), ((), ())), preferred_element_type=jnp.float32
        ).astype(jnp.bfloat16)


def weight_part(tops, grads):
    return pl.pallas_call(
        weight_kernel,
        out_shape=jax.ShapeDtypeStruct((tops[0].shape[1], grads[0].shape[1]), jnp.bfloat16),
        in_specs=[VMEM] * 8,
        out_specs=VMEM,
        compiler_params=params(32),
        name="weight_part",
    )(*tops, *grads)


def table_kernel(chunk, rb, ids_ref, x_ref, y_ref, o_ref):
    samples = x_ref.shape[0]
    one = jnp.ones((), jnp.bfloat16)
    zero = jnp.zeros((), jnp.bfloat16)
    target = lax.broadcasted_iota(jnp.int32, (rb, chunk), 0).astype(jnp.int16)

    def do_block(k, carry):
        base = k * rb
        acc = jnp.zeros((rb, x_ref.shape[1]), jnp.float32)
        for s in range(2 * samples // chunk):
            ids = (ids_ref[:, s * chunk : (s + 1) * chunk] - base).astype(jnp.int16)
            counts = None
            for j in range(ids_ref.shape[0]):
                hit = jnp.where(jnp.broadcast_to(ids[j : j + 1], (rb, chunk)) == target, one, zero)
                counts = hit if counts is None else counts + hit
            first = s * chunk
            rows = x_ref[first : first + chunk, :] if first < samples else y_ref[first - samples : first - samples + chunk, :]
            acc = acc + jnp.dot(counts, rows, preferred_element_type=jnp.float32)
        o_ref[pl.ds(pl.multiple_of(base, rb), rb), :] = acc.astype(jnp.bfloat16)
        return carry

    lax.fori_loop(0, o_ref.shape[0] // rb, do_block, 0)


def table_partial(ids, x, y):
    return pl.pallas_call(
        functools.partial(table_kernel, 256, 512),
        out_shape=jax.ShapeDtypeStruct((LOCAL_ROWS, x.shape[1]), jnp.bfloat16),
        in_specs=[VMEM] * 3,
        out_specs=VMEM,
        compiler_params=params(32),
        name="table_partial",
    )(ids, x, y)


def body(top_input, grad_hidden, w_in, b_in, slice_map, lookup_ids, bag_len):
    chip = lax.axis_index("chip")
    z, core = lax.div(chip, NC), lax.rem(chip, NC)
    bit = lax.rem(z, 2)
    b_dev, width = top_input.shape
    hidden = grad_hidden.shape[1]
    half = hidden // 2
    quart = half // NC

    top_core = core_swap(top_input)
    top_pair = pair_swap(top_input)

    grad_pre, ordered = front(slice_map, top_input, grad_hidden, w_in, b_in)

    keep = lax.dynamic_slice_in_dim(grad_pre, bit * half, half, 1)
    pair = pair_swap(lax.dynamic_slice_in_dim(grad_pre, (1 - bit) * half, half, 1))

    top_pair, pair = lax.optimization_barrier((top_pair, pair))
    piece = b_dev // 4
    top_both = jnp.concatenate(
        [core_swap(top_pair[k * piece : (k + 1) * piece]) for k in range(4)], axis=0
    )

    def mine(v):
        return lax.dynamic_slice_in_dim(v, core * quart, quart, 1)

    def other(v):
        return lax.dynamic_slice_in_dim(v, (1 - core) * quart, quart, 1)

    grads = (mine(keep), core_swap(other(keep)), mine(pair), core_swap(other(pair)))
    part = weight_part((top_input, top_core, top_pair, top_both), grads)

    received = lax.all_to_all(ordered, "hst", split_axis=0, concat_axis=1, tiled=True)[0]
    rec_other = core_swap(received)

    blocks = lax.all_to_all(
        part.reshape(NX * NY, width // (NX * NY), quart), "hst", split_axis=0, concat_axis=0, tiled=True
    )

    slots = lookup_ids.shape[1]
    ids = lookup_ids[0].reshape(slots, NX * NY, NZ, NC, b_dev)
    lens = bag_len[0].reshape(NX * NY, NZ, NC, b_dev)
    ids = lax.dynamic_index_in_dim(ids, z, 2, keepdims=False)
    lens = lax.dynamic_index_in_dim(lens, z, 1, keepdims=False)
    live = lax.iota(jnp.int32, slots)[:, None, None, None] < lens[None]
    here = (ids // ROWS_DEV) % NC == core
    local = (ids // (NC * ROWS_DEV)) * ROWS_DEV + ids % ROWS_DEV
    local = jnp.where(live & here, local, -1)
    near = lax.dynamic_index_in_dim(local, core, 2, keepdims=False).reshape(slots, -1)
    far = lax.dynamic_index_in_dim(local, 1 - core, 2, keepdims=False).reshape(slots, -1)
    local = jnp.concatenate([near, far], axis=1)
    table = table_partial(local, received, rec_other)
    table = table.reshape(NZ, ROWS_DEV, -1)

    def rows_of(d):
        return lax.dynamic_index_in_dim(table, lax.rem(z + d, NZ), 0, keepdims=False)

    table_grad = f32(rows_of(0))
    for d in (4, 3, 5, 2, 6, 1, 7):
        table_grad = table_grad + f32(z_shift(rows_of(d), d))

    summed = f32(blocks[0])
    for h in range(1, NX * NY):
        summed = summed + f32(blocks[h])
    summed = summed.astype(jnp.bfloat16)
    rows_out = summed.shape[0] // (NZ * NC)
    swapped = lax.all_to_all(
        summed.reshape(NZ * NC, rows_out, quart), "chip", split_axis=0, concat_axis=0, tiled=True
    )
    total = f32(swapped).reshape(NZ // 2, 2 * NC, rows_out, quart).sum(0)
    w_in_grad = total.transpose(1, 0, 2).reshape(rows_out, hidden)
    return (w_in_grad, table_grad[None])


def solution(mesh):
    in_specs = (
        P(("hst", "chip"), None),
        P(("hst", "chip"), None),
        P(),
        P(),
        P(),
        P("hst", None, None),
        P("hst", None),
    )
    out_specs = (P(("hst", "chip"), None), P("hst", "chip", None))
    return jax.shard_map(body, mesh=mesh, in_specs=in_specs, out_specs=out_specs, check_vma=False)
```

```python
import functools

import jax
import jax.numpy as jnp
from jax import lax
from jax.experimental import pallas as pl
from jax.experimental.pallas import tpu as pltpu
from jax.sharding import PartitionSpec as P

NX, NY, NZ, NC = 4, 4, 8, 2
AXES = ("hst", "chip")
ROWS_DEV = 256
LOCAL_ROWS = NZ * ROWS_DEV
VMEM = pl.BlockSpec(memory_space=pltpu.VMEM)
HBM = pl.BlockSpec(memory_space=pltpu.MemorySpace.HBM)


def device_index(x, y, z, c):
    return ((x * NY + y) * NZ + z) * NC + c


def permutation(target):
    pairs = []
    for x in range(NX):
        for y in range(NY):
            for z in range(NZ):
                for c in range(NC):
                    pairs.append((device_index(x, y, z, c), device_index(*target(x, y, z, c))))
    return pairs


def core_swap(value):
    return lax.ppermute(value, AXES, permutation(lambda x, y, z, c: (x, y, z, 1 - c)))


def pair_swap(value):
    return lax.ppermute(value, AXES, permutation(lambda x, y, z, c: (x, y, z ^ 1, c)))


def z_shift(value, d):
    return lax.ppermute(value, AXES, permutation(lambda x, y, z, c: (x, y, (z + d) % NZ, c)))


def f32(v):
    return v.astype(jnp.float32)


def in_hbm(v):
    return pltpu.with_memory_space_constraint(v, pltpu.MemorySpace.HBM)


def params(mib):
    return pltpu.CompilerParams(vmem_limit_bytes=mib << 20)


def front_kernel(map_hbm, top_hbm, gh_hbm, w_hbm, b_hbm, gp_ref, out_ref, map_ref, top_ref, gh_ref, w_ref, b_ref, acc_ref, sems):
    hidden = gh_ref.shape[1]
    blocks = sems.shape[0] - 4
    block = hidden // blocks
    small = [
        pltpu.make_async_copy(src, dst, sems.at[k])
        for k, (src, dst) in enumerate(
            ((top_hbm, top_ref), (b_hbm, b_ref), (gh_hbm, gh_ref), (map_hbm, map_ref))
        )
    ]
    large = [
        pltpu.make_async_copy(
            w_hbm.at[:, pl.ds(j * block, block)],
            w_ref.at[:, pl.ds(j * block, block)],
            sems.at[4 + j],
        )
        for j in range(blocks)
    ]
    for copy in small[:1] + large[:1] + small[1:] + large[1:]:
        copy.start()
    for j in range(blocks):
        cols = slice(j * block, (j + 1) * block)
        if j == 0:
            small[0].wait()
        large[j].wait()
        w = w_ref[:, cols]
        pre = jnp.dot(top_ref[...], w, preferred_element_type=jnp.float32)
        if j == 0:
            for copy in small[1:]:
                copy.wait()
        pre = pre + b_ref[:, cols]
        sig = 1.0 / (1.0 + jnp.exp(-pre))
        grad = (f32(gh_ref[:, cols]) * sig * (1.0 + pre * (1.0 - sig))).astype(jnp.bfloat16)
        gp_ref[:, cols] = grad
        part = lax.dot_general(grad, w, (((1,), (1,)), ((), ())), preferred_element_type=jnp.float32)
        if j == 0:
            acc_ref[...] = part
        else:
            acc_ref[...] += part
    slw = out_ref.shape[2]
    for s in range(out_ref.shape[0]):
        first = pl.multiple_of(map_ref[s] * slw, slw)
        out_ref[s] = acc_ref[:, pl.ds(first, slw)].astype(jnp.bfloat16)


def front(slice_map, top_input, grad_hidden, w_in, b_in, blocks=4):
    b_dev, width = top_input.shape
    hidden = grad_hidden.shape[1]
    slices = slice_map.shape[0]
    slw = width // slices
    return pl.pallas_call(
        front_kernel,
        in_specs=[HBM] * 5,
        out_specs=[VMEM] * 2,
        out_shape=[
            jax.ShapeDtypeStruct((b_dev, hidden), jnp.bfloat16),
            jax.ShapeDtypeStruct((slices, b_dev, slw), jnp.bfloat16),
        ],
        scratch_shapes=[
            pltpu.SMEM((slices,), jnp.int32),
            pltpu.VMEM((b_dev, width), jnp.bfloat16),
            pltpu.VMEM((b_dev, hidden), jnp.bfloat16),
            pltpu.VMEM((width, hidden), jnp.bfloat16),
            pltpu.VMEM((1, hidden), jnp.float32),
            pltpu.VMEM((b_dev, width), jnp.float32),
            pltpu.SemaphoreType.DMA((4 + blocks,)),
        ],
        compiler_params=params(20),
        name="front",
    )(*[in_hbm(v) for v in (slice_map, top_input, grad_hidden, w_in, b_in[None])])


def weight_kernel(x0, x1, x2, x3, g0, g1, g2, g3, o_ref):
    grads = jnp.concatenate([g[...] for g in (g0, g1, g2, g3)], axis=0)
    step = 512
    for first in range(0, x0.shape[1], step):
        left = jnp.concatenate([v[:, first : first + step] for v in (x0, x1, x2, x3)], axis=0)
        o_ref[first : first + step, :] = lax.dot_general(
            left, grads, (((0,), (0,)), ((), ())), preferred_element_type=jnp.float32
        ).astype(jnp.bfloat16)


def weight_part(tops, grads):
    return pl.pallas_call(
        weight_kernel,
        out_shape=jax.ShapeDtypeStruct((tops[0].shape[1], grads[0].shape[1]), jnp.bfloat16),
        in_specs=[VMEM] * 8,
        out_specs=VMEM,
        compiler_params=params(16),
        name="weight_part",
    )(*tops, *grads)


def sum_kernel(x_ref, o_ref):
    total = f32(x_ref[0])
    for k in range(1, x_ref.shape[0]):
        total = total + f32(x_ref[k])
    o_ref[...] = total.astype(o_ref.dtype)


def sum_blocks(blocks):
    return pl.pallas_call(
        sum_kernel,
        out_shape=jax.ShapeDtypeStruct(blocks.shape[1:], blocks.dtype),
        in_specs=[VMEM],
        out_specs=VMEM,
        compiler_params=params(8),
        name="sum_blocks",
    )(blocks)


def table_kernel(chunk, rb, ids_ref, x_hbm, y_hbm, o_ref, x_ref, y_ref, sems):
    copies = [
        pltpu.make_async_copy(x_hbm, x_ref, sems.at[0]),
        pltpu.make_async_copy(y_hbm, y_ref, sems.at[1]),
    ]
    for copy in copies:
        copy.start()
    for copy in copies:
        copy.wait()
    samples = x_ref.shape[0]
    one = jnp.ones((), jnp.bfloat16)
    zero = jnp.zeros((), jnp.bfloat16)
    target = lax.broadcasted_iota(jnp.int32, (rb, chunk), 0).astype(jnp.int16)

    def do_block(k, carry):
        base = k * rb
        acc = jnp.zeros((rb, x_ref.shape[1]), jnp.float32)
        for s in range(2 * samples // chunk):
            ids = (ids_ref[:, s * chunk : (s + 1) * chunk] - base).astype(jnp.int16)
            counts = None
            for j in range(ids_ref.shape[0]):
                hit = jnp.where(jnp.broadcast_to(ids[j : j + 1], (rb, chunk)) == target, one, zero)
                counts = hit if counts is None else counts + hit
            first = s * chunk
            rows = x_ref[first : first + chunk, :] if first < samples else y_ref[first - samples : first - samples + chunk, :]
            acc = acc + jnp.dot(counts, rows, preferred_element_type=jnp.float32)
        o_ref[pl.ds(pl.multiple_of(base, rb), rb), :] = acc.astype(jnp.bfloat16)
        return carry

    lax.fori_loop(0, o_ref.shape[0] // rb, do_block, 0)


def table_partial(ids, x, y):
    return pl.pallas_call(
        functools.partial(table_kernel, 256, 512),
        out_shape=jax.ShapeDtypeStruct((LOCAL_ROWS, x.shape[1]), jnp.bfloat16),
        in_specs=[VMEM, HBM, HBM],
        out_specs=VMEM,
        scratch_shapes=[
            pltpu.VMEM(x.shape, jnp.bfloat16),
            pltpu.VMEM(y.shape, jnp.bfloat16),
            pltpu.SemaphoreType.DMA((2,)),
        ],
        compiler_params=params(16),
        name="table_partial",
    )(ids, in_hbm(x), in_hbm(y))


def body(top_input, grad_hidden, w_in, b_in, slice_map, lookup_ids, bag_len):
    chip = lax.axis_index("chip")
    z, core = lax.div(chip, NC), lax.rem(chip, NC)
    bit = lax.rem(z, 2)
    b_dev, width = top_input.shape
    hidden = grad_hidden.shape[1]
    half = hidden // 2
    quart = half // NC

    top_core = core_swap(top_input)
    top_pair = pair_swap(top_input)

    grad_pre, ordered = front(slice_map, top_input, grad_hidden, w_in, b_in)

    keep = lax.dynamic_slice_in_dim(grad_pre, bit * half, half, 1)
    pair = pair_swap(lax.dynamic_slice_in_dim(grad_pre, (1 - bit) * half, half, 1))

    top_pair, pair = lax.optimization_barrier((top_pair, pair))
    piece = b_dev // 4
    top_both = jnp.concatenate(
        [core_swap(top_pair[k * piece : (k + 1) * piece]) for k in range(4)], axis=0
    )

    def mine(v):
        return lax.dynamic_slice_in_dim(v, core * quart, quart, 1)

    def other(v):
        return lax.dynamic_slice_in_dim(v, (1 - core) * quart, quart, 1)

    grads = (mine(keep), core_swap(other(keep)), mine(pair), core_swap(other(pair)))
    part = weight_part((top_input, top_core, top_pair, top_both), grads)

    received = lax.all_to_all(ordered, "hst", split_axis=0, concat_axis=1, tiled=True)[0]
    rec_other = core_swap(received)

    blocks = lax.all_to_all(
        part.reshape(NX * NY, width // (NX * NY), quart), "hst", split_axis=0, concat_axis=0, tiled=True
    )

    slots = lookup_ids.shape[1]
    ids = lookup_ids[0].reshape(slots, NX * NY, NZ, NC, b_dev)
    lens = bag_len[0].reshape(NX * NY, NZ, NC, b_dev)
    ids = lax.dynamic_index_in_dim(ids, z, 2, keepdims=False)
    lens = lax.dynamic_index_in_dim(lens, z, 1, keepdims=False)
    live = lax.iota(jnp.int32, slots)[:, None, None, None] < lens[None]
    here = (ids // ROWS_DEV) % NC == core
    local = (ids // (NC * ROWS_DEV)) * ROWS_DEV + ids % ROWS_DEV
    local = jnp.where(live & here, local, -1)
    near = lax.dynamic_index_in_dim(local, core, 2, keepdims=False).reshape(slots, -1)
    far = lax.dynamic_index_in_dim(local, 1 - core, 2, keepdims=False).reshape(slots, -1)
    local = jnp.concatenate([near, far], axis=1)
    table = table_partial(local, received, rec_other)
    table = table.reshape(NZ, ROWS_DEV, -1)

    def rows_of(d):
        return lax.dynamic_index_in_dim(table, lax.rem(z + d, NZ), 0, keepdims=False)

    table_grad = f32(rows_of(0))
    for d in (4, 3, 5, 2, 6, 1, 7):
        table_grad = table_grad + f32(z_shift(rows_of(d), d))

    summed = sum_blocks(blocks)
    rows_out = summed.shape[0] // (NZ * NC)
    swapped = lax.all_to_all(
        summed.reshape(NZ * NC, rows_out, quart), "chip", split_axis=0, concat_axis=0, tiled=True
    )
    total = f32(swapped).reshape(NZ // 2, 2 * NC, rows_out, quart).sum(0)
    w_in_grad = total.transpose(1, 0, 2).reshape(rows_out, hidden)
    return (w_in_grad, table_grad[None])


def solution(mesh):
    in_specs = (
        P(("hst", "chip"), None),
        P(("hst", "chip"), None),
        P(),
        P(),
        P(),
        P("hst", None, None),
        P("hst", None),
    )
    out_specs = (P(("hst", "chip"), None), P("hst", "chip", None))
    return jax.shard_map(body, mesh=mesh, in_specs=in_specs, out_specs=out_specs, check_vma=False)
```

```python
import functools

import jax
import jax.numpy as jnp
from jax import lax
from jax.experimental import pallas as pl
from jax.experimental.pallas import tpu as pltpu
from jax.sharding import PartitionSpec as P

NX, NY, NZ, NC = 4, 4, 8, 2
AXES = ("hst", "chip")
ROWS_DEV = 256
LOCAL_ROWS = NZ * ROWS_DEV
VMEM = pl.BlockSpec(memory_space=pltpu.VMEM)
HBM = pl.BlockSpec(memory_space=pltpu.MemorySpace.HBM)


def device_index(x, y, z, c):
    return ((x * NY + y) * NZ + z) * NC + c


def permutation(target):
    pairs = []
    for x in range(NX):
        for y in range(NY):
            for z in range(NZ):
                for c in range(NC):
                    pairs.append((device_index(x, y, z, c), device_index(*target(x, y, z, c))))
    return pairs


def core_swap(value):
    return lax.ppermute(value, AXES, permutation(lambda x, y, z, c: (x, y, z, 1 - c)))


def pair_swap(value):
    return lax.ppermute(value, AXES, permutation(lambda x, y, z, c: (x, y, z ^ 1, c)))


def z_shift(value, d):
    return lax.ppermute(value, AXES, permutation(lambda x, y, z, c: (x, y, (z + d) % NZ, c)))


def f32(v):
    return v.astype(jnp.float32)


def in_hbm(v):
    return pltpu.with_memory_space_constraint(v, pltpu.MemorySpace.HBM)


def params(mib):
    return pltpu.CompilerParams(vmem_limit_bytes=mib << 20)


def front_kernel(map_hbm, top_hbm, gh_hbm, w_hbm, b_hbm, keep_ref, give_ref, out_ref, map_ref, top_ref, gh_ref, w_ref, b_ref, gp_ref, acc_ref, sems):
    hidden = gh_ref.shape[1]
    blocks = sems.shape[0] - 4
    block = hidden // blocks
    small = [
        pltpu.make_async_copy(src, dst, sems.at[k])
        for k, (src, dst) in enumerate(
            ((top_hbm, top_ref), (b_hbm, b_ref), (gh_hbm, gh_ref), (map_hbm, map_ref))
        )
    ]
    large = [
        pltpu.make_async_copy(
            w_hbm.at[:, pl.ds(j * block, block)],
            w_ref.at[:, pl.ds(j * block, block)],
            sems.at[4 + j],
        )
        for j in range(blocks)
    ]
    for copy in small[:1] + large[:1] + small[1:] + large[1:]:
        copy.start()
    for j in range(blocks):
        cols = slice(j * block, (j + 1) * block)
        if j == 0:
            small[0].wait()
        large[j].wait()
        w = w_ref[:, cols]
        pre = jnp.dot(top_ref[...], w, preferred_element_type=jnp.float32)
        if j == 0:
            for copy in small[1:]:
                copy.wait()
        pre = pre + b_ref[:, cols]
        sig = 1.0 / (1.0 + jnp.exp(-pre))
        grad = (f32(gh_ref[:, cols]) * sig * (1.0 + pre * (1.0 - sig))).astype(jnp.bfloat16)
        gp_ref[:, cols] = grad
        part = lax.dot_general(grad, w, (((1,), (1,)), ((), ())), preferred_element_type=jnp.float32)
        if j == 0:
            acc_ref[...] = part
        else:
            acc_ref[...] += part
    bit = lax.rem(lax.div(lax.axis_index("chip"), NC), 2)
    half = hidden // 2
    keep_ref[...] = gp_ref[:, pl.ds(pl.multiple_of(bit * half, half), half)]
    give_ref[...] = gp_ref[:, pl.ds(pl.multiple_of((1 - bit) * half, half), half)]
    slw = out_ref.shape[2]
    for s in range(out_ref.shape[0]):
        first = pl.multiple_of(map_ref[s] * slw, slw)
        out_ref[s] = acc_ref[:, pl.ds(first, slw)].astype(jnp.bfloat16)


def front(slice_map, top_input, grad_hidden, w_in, b_in, blocks=4):
    b_dev, width = top_input.shape
    hidden = grad_hidden.shape[1]
    slices = slice_map.shape[0]
    slw = width // slices
    return pl.pallas_call(
        front_kernel,
        in_specs=[HBM] * 5,
        out_specs=[VMEM] * 3,
        out_shape=[
            jax.ShapeDtypeStruct((b_dev, hidden // 2), jnp.bfloat16),
            jax.ShapeDtypeStruct((b_dev, hidden // 2), jnp.bfloat16),
            jax.ShapeDtypeStruct((slices, b_dev, slw), jnp.bfloat16),
        ],
        scratch_shapes=[
            pltpu.SMEM((slices,), jnp.int32),
            pltpu.VMEM((b_dev, width), jnp.bfloat16),
            pltpu.VMEM((b_dev, hidden), jnp.bfloat16),
            pltpu.VMEM((width, hidden), jnp.bfloat16),
            pltpu.VMEM((1, hidden), jnp.float32),
            pltpu.VMEM((b_dev, hidden), jnp.bfloat16),
            pltpu.VMEM((b_dev, width), jnp.float32),
            pltpu.SemaphoreType.DMA((4 + blocks,)),
        ],
        compiler_params=params(20),
        name="front",
    )(*[in_hbm(v) for v in (slice_map, top_input, grad_hidden, w_in, b_in[None])])


def weight_kernel(x0, x1, x2, x3, g0, g1, g2, g3, o_ref):
    quart = o_ref.shape[1]
    core = lax.rem(lax.axis_index("chip"), NC)
    cols = pl.ds(pl.multiple_of(core * quart, quart), quart)
    grads = jnp.concatenate([g[:, cols] for g in (g0, g1, g2, g3)], axis=0)
    step = 512
    for first in range(0, x0.shape[1], step):
        left = jnp.concatenate([v[:, first : first + step] for v in (x0, x1, x2, x3)], axis=0)
        o_ref[first : first + step, :] = lax.dot_general(
            left, grads, (((0,), (0,)), ((), ())), preferred_element_type=jnp.float32
        ).astype(jnp.bfloat16)


def weight_part(tops, grads):
    return pl.pallas_call(
        weight_kernel,
        out_shape=jax.ShapeDtypeStruct((tops[0].shape[1], grads[0].shape[1] // NC), jnp.bfloat16),
        in_specs=[VMEM] * 8,
        out_specs=VMEM,
        compiler_params=params(16),
        name="weight_part",
    )(*tops, *grads)


def sum_kernel(x_ref, o_ref):
    total = f32(x_ref[0])
    for k in range(1, x_ref.shape[0]):
        total = total + f32(x_ref[k])
    o_ref[...] = total.astype(o_ref.dtype)


def sum_blocks(blocks):
    return pl.pallas_call(
        sum_kernel,
        out_shape=jax.ShapeDtypeStruct(blocks.shape[1:], blocks.dtype),
        in_specs=[VMEM],
        out_specs=VMEM,
        compiler_params=params(8),
        name="sum_blocks",
    )(blocks)


def table_kernel(chunk, rb, first, ids_ref, x_ref, *refs):
    o_ref = refs[-1]
    samples = x_ref.shape[0]
    one = jnp.ones((), jnp.bfloat16)
    zero = jnp.zeros((), jnp.bfloat16)
    target = lax.broadcasted_iota(jnp.int32, (rb, chunk), 0).astype(jnp.int16)

    def do_block(k, carry):
        base = k * rb
        rows = pl.ds(pl.multiple_of(base, rb), rb)
        if len(refs) > 1:
            acc = refs[0][rows, :]
        else:
            acc = jnp.zeros((rb, x_ref.shape[1]), jnp.float32)
        for s in range(samples // chunk):
            here = slice(first + s * chunk, first + (s + 1) * chunk)
            ids = (ids_ref[:, here] - base).astype(jnp.int16)
            counts = None
            for j in range(ids_ref.shape[0]):
                hit = jnp.where(jnp.broadcast_to(ids[j : j + 1], (rb, chunk)) == target, one, zero)
                counts = hit if counts is None else counts + hit
            acc = acc + jnp.dot(
                counts, x_ref[s * chunk : (s + 1) * chunk, :], preferred_element_type=jnp.float32
            )
        o_ref[rows, :] = acc.astype(o_ref.dtype)
        return carry

    lax.fori_loop(0, o_ref.shape[0] // rb, do_block, 0)


def table_partial(ids, x, sums=None):
    first = 0 if sums is None else x.shape[0]
    more = [] if sums is None else [sums]
    dtype = jnp.float32 if sums is None else jnp.bfloat16
    return pl.pallas_call(
        functools.partial(table_kernel, 256, 512, first),
        out_shape=jax.ShapeDtypeStruct((LOCAL_ROWS, x.shape[1]), dtype),
        in_specs=[VMEM] * (2 + len(more)),
        out_specs=VMEM,
        compiler_params=params(16),
        name="table_own" if sums is None else "table_other",
    )(ids, x, *more)


def last_kernel(w_ref, *refs):
    shares, w_out, t_out = refs[:-2], refs[-2], refs[-1]
    quart = w_ref.shape[2]
    parts = w_out.shape[1] // quart
    for q in range(parts):
        w_out[:, q * quart : (q + 1) * quart] = sum(
            f32(w_ref[k]) for k in range(q, w_ref.shape[0], parts)
        )
    t_out[...] = sum(f32(s[...]) for s in shares)


def last_sums(swapped, shares):
    _, rows, quart = swapped.shape
    return pl.pallas_call(
        last_kernel,
        out_shape=[
            jax.ShapeDtypeStruct((rows, 2 * NC * quart), jnp.float32),
            jax.ShapeDtypeStruct(shares[0].shape, jnp.float32),
        ],
        in_specs=[VMEM] * (1 + len(shares)),
        out_specs=[VMEM] * 2,
        compiler_params=params(8),
        name="last_sums",
    )(swapped, *shares)


def body(top_input, grad_hidden, w_in, b_in, slice_map, lookup_ids, bag_len):
    chip = lax.axis_index("chip")
    z, core = lax.div(chip, NC), lax.rem(chip, NC)
    b_dev, width = top_input.shape
    hidden = grad_hidden.shape[1]
    half = hidden // 2
    quart = half // NC

    top_core = core_swap(top_input)
    top_pair = pair_swap(top_input)

    keep, give, ordered = front(slice_map, top_input, grad_hidden, w_in, b_in)
    pair = pair_swap(give)

    top_pair, pair = lax.optimization_barrier((top_pair, pair))
    piece = b_dev // 4
    top_both = jnp.concatenate(
        [core_swap(top_pair[k * piece : (k + 1) * piece]) for k in range(4)], axis=0
    )

    grads = (keep, core_swap(keep), pair, core_swap(pair))

    slots = lookup_ids.shape[1]
    ids = lookup_ids[0].reshape(slots, NX * NY, NZ, NC, b_dev)
    lens = bag_len[0].reshape(NX * NY, NZ, NC, b_dev)
    ids = lax.dynamic_index_in_dim(ids, z, 2, keepdims=False)
    lens = lax.dynamic_index_in_dim(lens, z, 1, keepdims=False)
    live = lax.iota(jnp.int32, slots)[:, None, None, None] < lens[None]
    here = (ids // ROWS_DEV) % NC == core
    local = (ids // (NC * ROWS_DEV)) * ROWS_DEV + ids % ROWS_DEV
    local = jnp.where(live & here, local, -1)
    near = lax.dynamic_index_in_dim(local, core, 2, keepdims=False).reshape(slots, -1)
    far = lax.dynamic_index_in_dim(local, 1 - core, 2, keepdims=False).reshape(slots, -1)
    local = jnp.concatenate([near, far], axis=1)
    grads, local = lax.optimization_barrier((grads, local))
    part = weight_part((top_input, top_core, top_pair, top_both), grads)

    received = lax.all_to_all(ordered, "hst", split_axis=0, concat_axis=1, tiled=True)[0]
    rec_other = core_swap(received)

    blocks = lax.all_to_all(
        part.reshape(NX * NY, width // (NX * NY), quart), "hst", split_axis=0, concat_axis=0, tiled=True
    )

    table = table_partial(local, rec_other, table_partial(local, received))
    table = table.reshape(NZ, ROWS_DEV, -1)

    def rows_of(d):
        return lax.dynamic_index_in_dim(table, lax.rem(z + d, NZ), 0, keepdims=False)

    shares = [rows_of(0)] + [z_shift(rows_of(d), d) for d in (4, 3, 5, 2, 6, 1, 7)]

    blocks, shares = lax.optimization_barrier((blocks, shares))
    summed = sum_blocks(blocks)
    rows_out = summed.shape[0] // (NZ * NC)
    swapped = lax.all_to_all(
        summed.reshape(NZ * NC, rows_out, quart), "chip", split_axis=0, concat_axis=0, tiled=True
    )
    w_in_grad, table_grad = last_sums(swapped, shares)
    return (w_in_grad, table_grad[None])


def solution(mesh):
    in_specs = (
        P(("hst", "chip"), None),
        P(("hst", "chip"), None),
        P(),
        P(),
        P(),
        P("hst", None, None),
        P("hst", None),
    )
    out_specs = (P(("hst", "chip"), None), P("hst", "chip", None))
    return jax.shard_map(body, mesh=mesh, in_specs=in_specs, out_specs=out_specs, check_vma=False)
```

```python
import functools

import jax
import jax.numpy as jnp
from jax import lax
from jax.experimental import pallas as pl
from jax.experimental.pallas import tpu as pltpu
from jax.sharding import PartitionSpec as P

NX, NY, NZ, NC = 4, 4, 8, 2
AXES = ("hst", "chip")
ROWS_DEV = 256
FRONT_BLOCKS = (256, 256, 512, 512, 512)
LOCAL_ROWS = NZ * ROWS_DEV
VMEM = pl.BlockSpec(memory_space=pltpu.VMEM)
HBM = pl.BlockSpec(memory_space=pltpu.MemorySpace.HBM)


def device_index(x, y, z, c):
    return ((x * NY + y) * NZ + z) * NC + c


def permutation(target):
    pairs = []
    for x in range(NX):
        for y in range(NY):
            for z in range(NZ):
                for c in range(NC):
                    pairs.append((device_index(x, y, z, c), device_index(*target(x, y, z, c))))
    return pairs


def core_swap(value):
    return lax.ppermute(value, AXES, permutation(lambda x, y, z, c: (x, y, z, 1 - c)))


def pair_swap(value):
    return lax.ppermute(value, AXES, permutation(lambda x, y, z, c: (x, y, z ^ 1, c)))


def z_shift(value, d):
    return lax.ppermute(value, AXES, permutation(lambda x, y, z, c: (x, y, (z + d) % NZ, c)))


def f32(v):
    return v.astype(jnp.float32)


def in_hbm(v):
    return pltpu.with_memory_space_constraint(v, pltpu.MemorySpace.HBM)


def params(mib):
    return pltpu.CompilerParams(vmem_limit_bytes=mib << 20)


def front_kernel(map_hbm, top_hbm, gh_hbm, w_hbm, b_hbm, keep_ref, give_ref, out_ref, map_ref, top_ref, gh_ref, w_ref, b_ref, gp_ref, acc_ref, sems):
    hidden = gh_ref.shape[1]
    ends = [sum(FRONT_BLOCKS[: j + 1]) for j in range(len(FRONT_BLOCKS))]
    spans = [slice(end - size, end) for end, size in zip(ends, FRONT_BLOCKS)]
    small = [
        pltpu.make_async_copy(src, dst, sems.at[k])
        for k, (src, dst) in enumerate(
            ((top_hbm, top_ref), (b_hbm, b_ref), (gh_hbm, gh_ref), (map_hbm, map_ref))
        )
    ]
    large = [
        pltpu.make_async_copy(
            w_hbm.at[:, span],
            w_ref.at[:, span],
            sems.at[4 + j],
        )
        for j, span in enumerate(spans)
    ]
    for copy in small[:1] + large[:1] + small[1:] + large[1:]:
        copy.start()
    def cotangent(j):
        cols = spans[j]
        if j == 0:
            small[0].wait()
        large[j].wait()
        pre = jnp.dot(top_ref[...], w_ref[:, cols], preferred_element_type=jnp.float32)
        if j == 0:
            for copy in small[1:]:
                copy.wait()
        pre = pre + b_ref[:, cols]
        sig = 1.0 / (1.0 + jnp.exp(-pre))
        grad = (f32(gh_ref[:, cols]) * sig * (1.0 + pre * (1.0 - sig))).astype(jnp.bfloat16)
        gp_ref[:, cols] = grad
        return grad

    def back(j, grad):
        part = lax.dot_general(
            grad, w_ref[:, spans[j]], (((1,), (1,)), ((), ())), preferred_element_type=jnp.float32
        )
        if j == 0:
            acc_ref[...] = part
        else:
            acc_ref[...] += part

    grad = cotangent(0)
    for j in range(1, len(spans)):
        ahead = cotangent(j)
        back(j - 1, grad)
        grad = ahead
    back(len(spans) - 1, grad)
    bit = lax.rem(lax.div(lax.axis_index("chip"), NC), 2)
    half = hidden // 2
    keep_ref[...] = gp_ref[:, pl.ds(pl.multiple_of(bit * half, half), half)]
    give_ref[...] = gp_ref[:, pl.ds(pl.multiple_of((1 - bit) * half, half), half)]
    slw = out_ref.shape[2]
    for s in range(out_ref.shape[0]):
        first = pl.multiple_of(map_ref[s] * slw, slw)
        out_ref[s] = acc_ref[:, pl.ds(first, slw)].astype(jnp.bfloat16)


def front(slice_map, top_input, grad_hidden, w_in, b_in):
    b_dev, width = top_input.shape
    hidden = grad_hidden.shape[1]
    slices = slice_map.shape[0]
    slw = width // slices
    return pl.pallas_call(
        front_kernel,
        in_specs=[HBM] * 5,
        out_specs=[VMEM] * 3,
        out_shape=[
            jax.ShapeDtypeStruct((b_dev, hidden // 2), jnp.bfloat16),
            jax.ShapeDtypeStruct((b_dev, hidden // 2), jnp.bfloat16),
            jax.ShapeDtypeStruct((slices, b_dev, slw), jnp.bfloat16),
        ],
        scratch_shapes=[
            pltpu.SMEM((slices,), jnp.int32),
            pltpu.VMEM((b_dev, width), jnp.bfloat16),
            pltpu.VMEM((b_dev, hidden), jnp.bfloat16),
            pltpu.VMEM((width, hidden), jnp.bfloat16),
            pltpu.VMEM((1, hidden), jnp.float32),
            pltpu.VMEM((b_dev, hidden), jnp.bfloat16),
            pltpu.VMEM((b_dev, width), jnp.float32),
            pltpu.SemaphoreType.DMA((4 + len(FRONT_BLOCKS),)),
        ],
        compiler_params=params(20),
        name="front",
    )(*[in_hbm(v) for v in (slice_map, top_input, grad_hidden, w_in, b_in[None])])


def weight_kernel(x0, x1, x2, x3, g0, g1, g2, g3, o_ref):
    quart = o_ref.shape[1]
    core = lax.rem(lax.axis_index("chip"), NC)
    cols = pl.ds(pl.multiple_of(core * quart, quart), quart)
    grads = jnp.concatenate([g[:, cols] for g in (g0, g1, g2, g3)], axis=0)
    step = 512
    for first in range(0, x0.shape[1], step):
        left = jnp.concatenate([v[:, first : first + step] for v in (x0, x1, x2, x3)], axis=0)
        o_ref[first : first + step, :] = lax.dot_general(
            left, grads, (((0,), (0,)), ((), ())), preferred_element_type=jnp.float32
        ).astype(jnp.bfloat16)


def weight_part(tops, grads):
    return pl.pallas_call(
        weight_kernel,
        out_shape=jax.ShapeDtypeStruct((tops[0].shape[1], grads[0].shape[1] // NC), jnp.bfloat16),
        in_specs=[VMEM] * 8,
        out_specs=VMEM,
        compiler_params=params(16),
        name="weight_part",
    )(*tops, *grads)


def sum_kernel(x_ref, o_ref):
    total = f32(x_ref[0])
    for k in range(1, x_ref.shape[0]):
        total = total + f32(x_ref[k])
    o_ref[...] = total.astype(o_ref.dtype)


def sum_blocks(blocks):
    return pl.pallas_call(
        sum_kernel,
        out_shape=jax.ShapeDtypeStruct(blocks.shape[1:], blocks.dtype),
        in_specs=[VMEM],
        out_specs=VMEM,
        compiler_params=params(8),
        name="sum_blocks",
    )(blocks)


def table_kernel(chunk, rb, first, ids_ref, x_ref, *refs):
    o_ref = refs[-1]
    samples = x_ref.shape[0]
    one = jnp.ones((), jnp.bfloat16)
    zero = jnp.zeros((), jnp.bfloat16)
    target = lax.broadcasted_iota(jnp.int32, (rb, chunk), 0).astype(jnp.int16)

    def do_block(k, carry):
        base = k * rb
        rows = pl.ds(pl.multiple_of(base, rb), rb)
        if len(refs) > 1:
            acc = refs[0][rows, :]
        else:
            acc = jnp.zeros((rb, x_ref.shape[1]), jnp.float32)
        for s in range(samples // chunk):
            here = slice(first + s * chunk, first + (s + 1) * chunk)
            ids = (ids_ref[:, here] - base).astype(jnp.int16)
            counts = None
            for j in range(ids_ref.shape[0]):
                hit = jnp.where(jnp.broadcast_to(ids[j : j + 1], (rb, chunk)) == target, one, zero)
                counts = hit if counts is None else counts + hit
            acc = acc + jnp.dot(
                counts, x_ref[s * chunk : (s + 1) * chunk, :], preferred_element_type=jnp.float32
            )
        o_ref[rows, :] = acc.astype(o_ref.dtype)
        return carry

    lax.fori_loop(0, o_ref.shape[0] // rb, do_block, 0)


def table_partial(ids, x, sums=None):
    first = 0 if sums is None else x.shape[0]
    more = [] if sums is None else [sums]
    dtype = jnp.float32 if sums is None else jnp.bfloat16
    return pl.pallas_call(
        functools.partial(table_kernel, 256, 512, first),
        out_shape=jax.ShapeDtypeStruct((LOCAL_ROWS, x.shape[1]), dtype),
        in_specs=[VMEM] * (2 + len(more)),
        out_specs=VMEM,
        compiler_params=params(16),
        name="table_own" if sums is None else "table_other",
    )(ids, x, *more)


def last_kernel(w_ref, *refs):
    shares, w_out, t_out = refs[:-2], refs[-2], refs[-1]
    quart = w_ref.shape[2]
    parts = w_out.shape[1] // quart
    for q in range(parts):
        w_out[:, q * quart : (q + 1) * quart] = sum(
            f32(w_ref[k]) for k in range(q, w_ref.shape[0], parts)
        )
    t_out[...] = sum(f32(s[...]) for s in shares)


def last_sums(swapped, shares):
    _, rows, quart = swapped.shape
    return pl.pallas_call(
        last_kernel,
        out_shape=[
            jax.ShapeDtypeStruct((rows, 2 * NC * quart), jnp.float32),
            jax.ShapeDtypeStruct(shares[0].shape, jnp.float32),
        ],
        in_specs=[VMEM] * (1 + len(shares)),
        out_specs=[VMEM] * 2,
        compiler_params=params(8),
        name="last_sums",
    )(swapped, *shares)


def body(top_input, grad_hidden, w_in, b_in, slice_map, lookup_ids, bag_len):
    chip = lax.axis_index("chip")
    z, core = lax.div(chip, NC), lax.rem(chip, NC)
    b_dev, width = top_input.shape
    hidden = grad_hidden.shape[1]
    half = hidden // 2
    quart = half // NC

    top_core = core_swap(top_input)
    top_pair = pair_swap(top_input)

    keep, give, ordered = front(slice_map, top_input, grad_hidden, w_in, b_in)
    pair = pair_swap(give)

    top_pair, pair = lax.optimization_barrier((top_pair, pair))
    piece = b_dev // 4
    top_both = jnp.concatenate(
        [core_swap(top_pair[k * piece : (k + 1) * piece]) for k in range(4)], axis=0
    )

    grads = (keep, core_swap(keep), pair, core_swap(pair))

    slots = lookup_ids.shape[1]
    ids = lookup_ids[0].reshape(slots, NX * NY, NZ, NC, b_dev)
    lens = bag_len[0].reshape(NX * NY, NZ, NC, b_dev)
    ids = lax.dynamic_index_in_dim(ids, z, 2, keepdims=False)
    lens = lax.dynamic_index_in_dim(lens, z, 1, keepdims=False)
    live = lax.iota(jnp.int32, slots)[:, None, None, None] < lens[None]
    here = (ids // ROWS_DEV) % NC == core
    local = (ids // (NC * ROWS_DEV)) * ROWS_DEV + ids % ROWS_DEV
    local = jnp.where(live & here, local, -1)
    near = lax.dynamic_index_in_dim(local, core, 2, keepdims=False).reshape(slots, -1)
    far = lax.dynamic_index_in_dim(local, 1 - core, 2, keepdims=False).reshape(slots, -1)
    local = jnp.concatenate([near, far], axis=1)
    part = weight_part((top_input, top_core, top_pair, top_both), grads)

    received = lax.all_to_all(ordered, "hst", split_axis=0, concat_axis=1, tiled=True)[0]
    rec_other = core_swap(received)

    blocks = lax.all_to_all(
        part.reshape(NX * NY, width // (NX * NY), quart), "hst", split_axis=0, concat_axis=0, tiled=True
    )

    table = table_partial(local, rec_other, table_partial(local, received))
    table = table.reshape(NZ, ROWS_DEV, -1)

    def rows_of(d):
        return lax.dynamic_index_in_dim(table, lax.rem(z + d, NZ), 0, keepdims=False)

    shares = [rows_of(0)] + [z_shift(rows_of(d), d) for d in (4, 3, 5, 2, 6, 1, 7)]

    blocks, shares = lax.optimization_barrier((blocks, shares))
    summed = sum_blocks(blocks)
    rows_out = summed.shape[0] // (NZ * NC)
    swapped = lax.all_to_all(
        summed.reshape(NZ * NC, rows_out, quart), "chip", split_axis=0, concat_axis=0, tiled=True
    )
    w_in_grad, table_grad = last_sums(swapped, shares)
    return (w_in_grad, table_grad[None])


def solution(mesh):
    in_specs = (
        P(("hst", "chip"), None),
        P(("hst", "chip"), None),
        P(),
        P(),
        P(),
        P("hst", None, None),
        P("hst", None),
    )
    out_specs = (P(("hst", "chip"), None), P("hst", "chip", None))
    return jax.shard_map(body, mesh=mesh, in_specs=in_specs, out_specs=out_specs, check_vma=False)
```

```python
import functools

import jax
import jax.numpy as jnp
from jax import lax
from jax.experimental import pallas as pl
from jax.experimental.pallas import tpu as pltpu
from jax.sharding import PartitionSpec as P

NX, NY, NZ, NC = 4, 4, 8, 2
AXES = ("hst", "chip")
ROWS_DEV = 256
FRONT_BLOCKS = (256, 256, 512, 512, 512)
LOCAL_ROWS = NZ * ROWS_DEV
VMEM = pl.BlockSpec(memory_space=pltpu.VMEM)
HBM = pl.BlockSpec(memory_space=pltpu.MemorySpace.HBM)


def device_index(x, y, z, c):
    return ((x * NY + y) * NZ + z) * NC + c


def permutation(target):
    pairs = []
    for x in range(NX):
        for y in range(NY):
            for z in range(NZ):
                for c in range(NC):
                    pairs.append((device_index(x, y, z, c), device_index(*target(x, y, z, c))))
    return pairs


def core_swap(value):
    return lax.ppermute(value, AXES, permutation(lambda x, y, z, c: (x, y, z, 1 - c)))


def pair_swap(value):
    return lax.ppermute(value, AXES, permutation(lambda x, y, z, c: (x, y, z ^ 1, c)))


def z_shift(value, d):
    return lax.ppermute(value, AXES, permutation(lambda x, y, z, c: (x, y, (z + d) % NZ, c)))


def f32(v):
    return v.astype(jnp.float32)


def in_hbm(v):
    return pltpu.with_memory_space_constraint(v, pltpu.MemorySpace.HBM)


def params(mib):
    return pltpu.CompilerParams(vmem_limit_bytes=mib << 20)


def front_kernel(map_hbm, top_hbm, gh_hbm, w_hbm, b_hbm, keep_ref, give_ref, out_ref, map_ref, top_ref, gh_ref, w_ref, b_ref, gp_ref, acc_ref, sems):
    hidden = gh_ref.shape[1]
    ends = [sum(FRONT_BLOCKS[: j + 1]) for j in range(len(FRONT_BLOCKS))]
    spans = [slice(end - size, end) for end, size in zip(ends, FRONT_BLOCKS)]
    small = [
        pltpu.make_async_copy(src, dst, sems.at[k])
        for k, (src, dst) in enumerate(
            ((top_hbm, top_ref), (b_hbm, b_ref), (gh_hbm, gh_ref), (map_hbm, map_ref))
        )
    ]
    large = [
        pltpu.make_async_copy(
            w_hbm.at[:, span],
            w_ref.at[:, span],
            sems.at[4 + j],
        )
        for j, span in enumerate(spans)
    ]
    for copy in small[:1] + large[:1] + small[1:] + large[1:]:
        copy.start()
    def cotangent(j):
        cols = spans[j]
        if j == 0:
            small[0].wait()
        large[j].wait()
        pre = jnp.dot(top_ref[...], w_ref[:, cols], preferred_element_type=jnp.float32)
        if j == 0:
            for copy in small[1:]:
                copy.wait()
        pre = pre + b_ref[:, cols]
        sig = 1.0 / (1.0 + jnp.exp(-pre))
        grad = (f32(gh_ref[:, cols]) * sig * (1.0 + pre * (1.0 - sig))).astype(jnp.bfloat16)
        gp_ref[:, cols] = grad
        return grad

    def back(j, grad):
        part = lax.dot_general(
            grad, w_ref[:, spans[j]], (((1,), (1,)), ((), ())), preferred_element_type=jnp.float32
        )
        if j == 0:
            acc_ref[...] = part
        else:
            acc_ref[...] += part

    grad = cotangent(0)
    for j in range(1, len(spans)):
        ahead = cotangent(j)
        back(j - 1, grad)
        grad = ahead
    back(len(spans) - 1, grad)
    bit = lax.rem(lax.div(lax.axis_index("chip"), NC), 2)
    half = hidden // 2
    keep_ref[...] = gp_ref[:, pl.ds(pl.multiple_of(bit * half, half), half)]
    give_ref[...] = gp_ref[:, pl.ds(pl.multiple_of((1 - bit) * half, half), half)]
    slw = out_ref.shape[2]
    for s in range(out_ref.shape[0]):
        first = pl.multiple_of(map_ref[s] * slw, slw)
        out_ref[s] = acc_ref[:, pl.ds(first, slw)].astype(jnp.bfloat16)


def front(slice_map, top_input, grad_hidden, w_in, b_in):
    b_dev, width = top_input.shape
    hidden = grad_hidden.shape[1]
    slices = slice_map.shape[0]
    slw = width // slices
    return pl.pallas_call(
        front_kernel,
        in_specs=[HBM] * 5,
        out_specs=[VMEM] * 3,
        out_shape=[
            jax.ShapeDtypeStruct((b_dev, hidden // 2), jnp.bfloat16),
            jax.ShapeDtypeStruct((b_dev, hidden // 2), jnp.bfloat16),
            jax.ShapeDtypeStruct((slices, b_dev, slw), jnp.bfloat16),
        ],
        scratch_shapes=[
            pltpu.SMEM((slices,), jnp.int32),
            pltpu.VMEM((b_dev, width), jnp.bfloat16),
            pltpu.VMEM((b_dev, hidden), jnp.bfloat16),
            pltpu.VMEM((width, hidden), jnp.bfloat16),
            pltpu.VMEM((1, hidden), jnp.float32),
            pltpu.VMEM((b_dev, hidden), jnp.bfloat16),
            pltpu.VMEM((b_dev, width), jnp.float32),
            pltpu.SemaphoreType.DMA((4 + len(FRONT_BLOCKS),)),
        ],
        compiler_params=params(20),
        name="front",
    )(*[in_hbm(v) for v in (slice_map, top_input, grad_hidden, w_in, b_in[None])])


def weight_kernel(x0, x1, x2, x3, g0, g1, g2, g3, o_ref):
    quart = o_ref.shape[1]
    core = lax.rem(lax.axis_index("chip"), NC)
    cols = pl.ds(pl.multiple_of(core * quart, quart), quart)
    grads = jnp.concatenate([g[:, cols] for g in (g0, g1, g2, g3)], axis=0)
    step = 512
    for first in range(0, x0.shape[1], step):
        left = jnp.concatenate([v[:, first : first + step] for v in (x0, x1, x2, x3)], axis=0)
        o_ref[first : first + step, :] = lax.dot_general(
            left, grads, (((0,), (0,)), ((), ())), preferred_element_type=jnp.float32
        ).astype(jnp.bfloat16)


def weight_part(tops, grads):
    return pl.pallas_call(
        weight_kernel,
        out_shape=jax.ShapeDtypeStruct((tops[0].shape[1], grads[0].shape[1] // NC), jnp.bfloat16),
        in_specs=[VMEM] * 8,
        out_specs=VMEM,
        compiler_params=params(16),
        name="weight_part",
    )(*tops, *grads)


def sum_kernel(x_ref, o_ref):
    total = f32(x_ref[0])
    for k in range(1, x_ref.shape[0]):
        total = total + f32(x_ref[k])
    o_ref[...] = total.astype(o_ref.dtype)


def sum_blocks(blocks):
    return pl.pallas_call(
        sum_kernel,
        out_shape=jax.ShapeDtypeStruct(blocks.shape[1:], blocks.dtype),
        in_specs=[VMEM],
        out_specs=VMEM,
        compiler_params=params(8),
        name="sum_blocks",
    )(blocks)


def table_kernel(chunk, rb, first, ids_ref, x_ref, *refs):
    o_ref = refs[-1]
    samples = x_ref.shape[0]
    one = jnp.ones((), jnp.bfloat16)
    zero = jnp.zeros((), jnp.bfloat16)
    target = lax.broadcasted_iota(jnp.int32, (rb, chunk), 0).astype(jnp.int16)

    def do_block(k, carry):
        base = k * rb
        rows = pl.ds(pl.multiple_of(base, rb), rb)
        if len(refs) > 1:
            acc = refs[0][rows, :]
        else:
            acc = jnp.zeros((rb, x_ref.shape[1]), jnp.float32)
        for s in range(samples // chunk):
            here = slice(first + s * chunk, first + (s + 1) * chunk)
            ids = (ids_ref[:, here] - base).astype(jnp.int16)
            counts = None
            for j in range(ids_ref.shape[0]):
                hit = jnp.where(jnp.broadcast_to(ids[j : j + 1], (rb, chunk)) == target, one, zero)
                counts = hit if counts is None else counts + hit
            acc = acc + jnp.dot(
                counts, x_ref[s * chunk : (s + 1) * chunk, :], preferred_element_type=jnp.float32
            )
        o_ref[rows, :] = acc.astype(o_ref.dtype)
        return carry

    lax.fori_loop(0, o_ref.shape[0] // rb, do_block, 0)


def table_partial(ids, x, sums=None):
    first = 0 if sums is None else x.shape[0]
    more = [] if sums is None else [sums]
    dtype = jnp.float32 if sums is None else jnp.bfloat16
    return pl.pallas_call(
        functools.partial(table_kernel, 256, 512, first),
        out_shape=jax.ShapeDtypeStruct((LOCAL_ROWS, x.shape[1]), dtype),
        in_specs=[VMEM] * (2 + len(more)),
        out_specs=VMEM,
        compiler_params=params(16),
        name="table_own" if sums is None else "table_other",
    )(ids, x, *more)


def last_kernel(w_ref, *refs):
    shares, w_out, t_out = refs[:-2], refs[-2], refs[-1]
    quart = w_ref.shape[2]
    parts = w_out.shape[1] // quart
    for q in range(parts):
        w_out[:, q * quart : (q + 1) * quart] = sum(
            f32(w_ref[k]) for k in range(q, w_ref.shape[0], parts)
        )
    t_out[...] = sum(f32(s[...]) for s in shares)


def last_sums(swapped, shares):
    _, rows, quart = swapped.shape
    return pl.pallas_call(
        last_kernel,
        out_shape=[
            jax.ShapeDtypeStruct((rows, 2 * NC * quart), jnp.float32),
            jax.ShapeDtypeStruct(shares[0].shape, jnp.float32),
        ],
        in_specs=[VMEM] * (1 + len(shares)),
        out_specs=[VMEM] * 2,
        compiler_params=params(8),
        name="last_sums",
    )(swapped, *shares)


def body(top_input, grad_hidden, w_in, b_in, slice_map, lookup_ids, bag_len):
    chip = lax.axis_index("chip")
    z, core = lax.div(chip, NC), lax.rem(chip, NC)
    b_dev, width = top_input.shape
    hidden = grad_hidden.shape[1]
    half = hidden // 2
    quart = half // NC

    top_core = core_swap(top_input)
    top_pair = pair_swap(top_input)

    keep, give, ordered = front(slice_map, top_input, grad_hidden, w_in, b_in)
    pair = pair_swap(give)

    top_pair, pair = lax.optimization_barrier((top_pair, pair))
    piece = b_dev // 2
    top_both = jnp.concatenate(
        [core_swap(top_pair[k * piece : (k + 1) * piece]) for k in range(2)], axis=0
    )

    grads = (keep, core_swap(keep), pair, core_swap(pair))

    slots = lookup_ids.shape[1]
    ids = lookup_ids[0].reshape(slots, NX * NY, NZ, NC, b_dev)
    lens = bag_len[0].reshape(NX * NY, NZ, NC, b_dev)
    ids = lax.dynamic_index_in_dim(ids, z, 2, keepdims=False)
    lens = lax.dynamic_index_in_dim(lens, z, 1, keepdims=False)
    live = lax.iota(jnp.int32, slots)[:, None, None, None] < lens[None]
    here = (ids // ROWS_DEV) % NC == core
    local = (ids // (NC * ROWS_DEV)) * ROWS_DEV + ids % ROWS_DEV
    local = jnp.where(live & here, local, -1)
    near = lax.dynamic_index_in_dim(local, core, 2, keepdims=False).reshape(slots, -1)
    far = lax.dynamic_index_in_dim(local, 1 - core, 2, keepdims=False).reshape(slots, -1)
    local = jnp.concatenate([near, far], axis=1)
    part = weight_part((top_input, top_core, top_pair, top_both), grads)

    received = lax.all_to_all(ordered, "hst", split_axis=0, concat_axis=1, tiled=True)[0]
    rec_other = core_swap(received)

    blocks = lax.all_to_all(
        part.reshape(NX * NY, width // (NX * NY), quart), "hst", split_axis=0, concat_axis=0, tiled=True
    )

    table = table_partial(local, rec_other, table_partial(local, received))
    table = table.reshape(NZ, ROWS_DEV, -1)

    def rows_of(d):
        return lax.dynamic_index_in_dim(table, lax.rem(z + d, NZ), 0, keepdims=False)

    shares = [rows_of(0)] + [z_shift(rows_of(d), d) for d in (4, 3, 5, 2, 6, 1, 7)]

    blocks, shares = lax.optimization_barrier((blocks, shares))
    summed = sum_blocks(blocks)
    rows_out = summed.shape[0] // (NZ * NC)
    swapped = lax.all_to_all(
        summed.reshape(NZ * NC, rows_out, quart), "chip", split_axis=0, concat_axis=0, tiled=True
    )
    w_in_grad, table_grad = last_sums(swapped, shares)
    return (w_in_grad, table_grad[None])


def solution(mesh):
    in_specs = (
        P(("hst", "chip"), None),
        P(("hst", "chip"), None),
        P(),
        P(),
        P(),
        P("hst", None, None),
        P("hst", None),
    )
    out_specs = (P(("hst", "chip"), None), P("hst", "chip", None))
    return jax.shard_map(body, mesh=mesh, in_specs=in_specs, out_specs=out_specs, check_vma=False)
```
